256 devices in a mesh: dp: 32 (over z_lo, x, y), seq: 4 (over z_hi), fsdp: 2 (over core).
Axes of the slice: x: 4, y: 4, z: 8 (z_hi: 4, z_lo: 2; z = z_hi * 2 + z_lo), core: 2. Of those that a mesh axis runs over, the one named last changes fastest.
Arguments:
- layer_input: bfloat16 [64, 512, 5120], P(('dp', 'fsdp'), 'seq'), may hold values from -16 to 16
- query: bfloat16 [64, 512, 2560], P(('dp', 'fsdp'), 'seq'), may hold values from -24 to 24
- out_grad: bfloat16 [64, 512, 2560], P(('dp', 'fsdp'), 'seq'), may hold values from -6 to 6
- camera_counts: int32 [64, 1], P(('dp', 'fsdp')), may hold values from 1 to 3
- action_counts: int32 [64, 1], P(('dp', 'fsdp')), may hold values from 20 to 60
- kv_weight: bfloat16 [5120, 1024], P('fsdp'), may hold values from -0.078125 to 0.078125
Outputs:
- input_grad: bfloat16 [64, 512, 5120], P(('dp', 'fsdp'), 'seq')
- weight_grad: float32 [5120, 1024], P(('dp', 'fsdp'), 'seq')
The draws below stay inside these ranges and needn't reach their ends.
All inputs are finite; a program needn't handle non-finite values.
Results may differ from the reference program's by a relative error of at most 0.011.
Values may be sent and summed in bfloat16 or wider, within the bound.
No kernel may reach another device: no remote copies, remote signals or barrier semaphores. Data moves between devices by JAX's collectives and lax.ppermute only.
A program may use at most 128 MiB of HBM per device.

```python
import jax
import jax.numpy as jnp
from jax import lax

D = 5120
QH = 20
KVH = 4
HD = 128
IMG_TOK = 64
TEXT = 32
AMIN = 20
CAMS = 3
SEQ = 512
ROWS = 64
KVC = 1024
SAMPLES = 1


def draw_query(key, part):
    key = jax.random.fold_in(key, 11)
    normals = jax.random.truncated_normal(key, -6.0, 6.0, (ROWS, SEQ, QH * HD), jnp.float32)
    return normals.astype(jnp.bfloat16)


def touch_ends(drawn, key, smallest, high):
    longest = drawn.shape.index(max(drawn.shape))
    spots = []
    for shift in (0, 1):
        where = [jax.random.randint(jax.random.fold_in(key, axis), (), 0, length) for axis, length in enumerate(drawn.shape)]
        where[longest] = (where[longest] + shift) % drawn.shape[longest]
        spots.append(tuple(where))
    return drawn.at[spots[0]].set(smallest).at[spots[1]].set(high)


def spiked(result, own_key, source, target, blocks, factor):
    owner, partner = [(jnp.arange(result.shape[axis_at]) // (result.shape[axis_at] // blocks)).reshape([-1 if axis == axis_at else 1 for axis in range(result.ndim)]) for axis_at in (source, target)]
    chosen = jax.random.permutation(own_key, blocks)[partner]
    strong = (owner == chosen) | (owner == (partner + blocks // 2) % blocks)
    return jnp.where(strong, factor * result, result)


def levels(key, dims, pieces, low, largest):
    level, own = 1.0, jax.random.fold_in(key, 6)
    for dim, parts in pieces:
        steps = jnp.exp(jax.random.uniform(jax.random.fold_in(own, dim), (parts,), jnp.float32, low / len(pieces), largest / len(pieces)))
        level = level * jnp.repeat(steps, dims[dim] // parts).reshape([-1 if axis == dim else 1 for axis in range(len(dims))])
    return level


def scatter_about(key, shape, scale, reach, split=(), held_as=jnp.bfloat16):
    result = scale * jax.random.normal(key, shape, jnp.float32)
    if split:
        result = result * levels(key, shape, split, -0.22, 0.18)
    return jnp.clip(result, -reach, reach).astype(held_as)


def bell_draw_with(key, shape, scale, most, shards, heavy, kind=jnp.bfloat16):
    result = scale * jax.random.normal(key, shape, jnp.float32)
    if shards:
        result = result * levels(key, shape, shards, -0.22, 0.18)
    return jnp.clip(spiked(result, jax.random.fold_in(key, 3), *heavy), -most, most).astype(kind)


def setup_inputs(seed: int = 0) -> dict:
    splits = jax.random.split(jax.random.key(seed), 7)
    return {
        "layer_input": bell_draw_with(splits[0], (ROWS, SEQ, D), 1.0, 16.0, ((0, 64), (1, 4)), (0, 2, 64, 4.0)),
        "query": draw_query(jax.random.fold_in(splits[6], 71), 0),
        "out_grad": scatter_about(splits[2], (ROWS, SEQ, QH * HD), 1.0, 6.0, ((0, 64), (1, 4))),
        "camera_counts": touch_ends(jax.random.randint(splits[3], (ROWS, SAMPLES), 1, CAMS + 1), jax.random.fold_in(splits[3], 1), 1, CAMS).astype(jnp.int32),
        "action_counts": touch_ends(jax.random.randint(splits[4], (ROWS, SAMPLES), AMIN, 3 * AMIN + 1), jax.random.fold_in(splits[4], 1), AMIN, 3 * AMIN).astype(jnp.int32),
        "kv_weight": scatter_about(splits[5], (D, KVC), D ** -0.5, 0.078125, ((0, 2),)),
    }


rope_base = 1000000.0
neg_fill = -1.0e30


def token_layout(cameras, actions, length):
    prefix_sizes = (cameras * IMG_TOK + TEXT).astype(jnp.int32)
    sample_sizes = (prefix_sizes + actions).astype(jnp.int32)
    sample_ends = jnp.cumsum(sample_sizes).astype(jnp.int32)
    sample_starts = (sample_ends - sample_sizes).astype(jnp.int32)
    places = jnp.arange(length, dtype=jnp.int32)
    segment = jnp.sum((places[:, None] >= sample_ends[None, :]).astype(jnp.int32), axis=1).astype(jnp.int32)
    firsts = jnp.concatenate([sample_starts, sample_ends[-1:]]).astype(jnp.int32)
    limits = jnp.concatenate([prefix_sizes, jnp.full((1,), length, jnp.int32)]).astype(jnp.int32)
    labels = jnp.arange(firsts.shape[0], dtype=jnp.int32)
    onehot = segment[:, None] == labels[None, :]
    row_first = jnp.sum(jnp.where(onehot, firsts[None, :], 0), axis=1).astype(jnp.int32)
    bounds = jnp.sum(jnp.where(onehot, limits[None, :], 0), axis=1).astype(jnp.int32)
    return segment, (places - row_first).astype(jnp.int32), bounds


def rope_tables(position):
    frequency = rope_base ** (-(2.0 * jnp.arange(HD // 2, dtype=jnp.float32)) / HD)
    angles = position.astype(jnp.float32)[:, None] * frequency[None, :]
    return jnp.cos(angles), jnp.sin(angles)


def rotate(values_in, cos_table, sin_table):
    half_width = HD // 2
    lower_half = values_in[..., :half_width]
    upper_half = values_in[..., half_width:]
    cosines = cos_table[:, None, :]
    sine_part = sin_table[:, None, :]
    return jnp.concatenate([lower_half * cosines - upper_half * sine_part, upper_half * cosines + lower_half * sine_part], axis=-1)


def unrotate(values_in, cos_table, sin_table):
    half_width = HD // 2
    lower_half = values_in[..., :half_width]
    upper_half = values_in[..., half_width:]
    cosines = cos_table[:, None, :]
    sine_part = sin_table[:, None, :]
    return jnp.concatenate([lower_half * cosines + upper_half * sine_part, upper_half * cosines - lower_half * sine_part], axis=-1)


def attend_mask(query_segment, query_position, key_segment, key_position, key_bounds):
    same_sample = query_segment[:, None] == key_segment[None, :]
    visible = (key_position < key_bounds)[None, :] | (key_position[None, :] <= query_position[:, None])
    return same_sample & visible


def row_terms(layer_row, query_row, grad_row, cameras, actions, kv_weight):
    length = layer_row.shape[0]
    group_size = QH // KVH
    segment, position, bounds = token_layout(cameras, actions, length)
    cos_table, sin_table = rope_tables(position)
    projected = jnp.dot(layer_row, kv_weight, preferred_element_type=jnp.float32).reshape(length, KVH, 2, HD)
    keys_rot = rotate(projected[:, :, 0], cos_table, sin_table).astype(jnp.bfloat16)
    values_all = projected[:, :, 1].astype(jnp.bfloat16)
    live_rows = (segment < cameras.shape[0])[:, None]
    grad_rows = jnp.where(live_rows, grad_row, jnp.zeros_like(grad_row))
    queries = query_row.reshape(length, KVH, group_size, HD).astype(jnp.float32)
    grads = grad_rows.reshape(length, KVH, group_size, HD).astype(jnp.float32)
    keys_wide = keys_rot.astype(jnp.float32)
    values_wide = values_all.astype(jnp.float32)
    score_scale = HD ** -0.5
    allowed = attend_mask(segment, position, segment, position, bounds)
    scores = jnp.einsum("qhgd,khd->hgqk", queries, keys_wide) * score_scale
    masked = jnp.where(allowed, scores, neg_fill)
    row_top = jnp.max(masked, axis=-1, keepdims=True)
    exponent = jnp.exp(masked - row_top)
    attention = exponent / jnp.sum(exponent, axis=-1, keepdims=True)
    grad_attention = jnp.einsum("qhgd,khd->hgqk", grads, values_wide)
    row_delta = jnp.sum(attention * grad_attention, axis=-1, keepdims=True)
    grad_scores = lax.optimization_barrier((attention * (grad_attention - row_delta)).astype(jnp.bfloat16)).astype(jnp.float32)
    attention_low = lax.optimization_barrier(attention.astype(jnp.bfloat16)).astype(jnp.float32)
    grad_values = jnp.einsum("hgqk,qhgd->khd", attention_low, grads)
    grad_rot = jnp.einsum("hgqk,qhgd->khd", grad_scores, queries) * score_scale
    grad_keys = unrotate(grad_rot, cos_table, sin_table)
    key_grads = jnp.stack([grad_keys, grad_values], axis=2).reshape(length, KVH * 2 * HD).astype(jnp.bfloat16)
    input_row = jnp.dot(key_grads, kv_weight.T, preferred_element_type=jnp.float32).astype(jnp.bfloat16)
    weight_row = jnp.dot(layer_row.T, key_grads, preferred_element_type=jnp.float32)
    return input_row, weight_row


def reference(layer_input, query, out_grad, camera_counts, action_counts, kv_weight):
    def scan_step(running, row_items):
        layer_row, query_row, grad_row, cameras, actions = row_items
        input_row, weight_row = row_terms(layer_row, query_row, grad_row, cameras, actions, kv_weight)
        return running + weight_row, input_row

    initial = jnp.zeros((D, KVC), jnp.float32)
    running, input_grad = lax.scan(scan_step, initial, (layer_input, query, out_grad, camera_counts, action_counts))
    return input_grad, running / ROWS
```

```python
import functools

import jax
import jax.numpy as jnp
from jax import lax
from jax.experimental import pallas as pl
from jax.experimental.pallas import tpu as pltpu
from jax.sharding import PartitionSpec as P

HD = 128
GROUP = 5
KVH = 4
IMG_TOK = 64
TEXT = 32
TOK = 128
rope_base = 1000000.0
neg_fill = -1e30
far_away = 1 << 20
NC = 1
VMEM = pl.BlockSpec(memory_space=pltpu.VMEM)
SMEM = pl.BlockSpec(memory_space=pltpu.SMEM)
PARAMS = pltpu.CompilerParams(vmem_limit_bytes=48 * 1024 * 1024)
F32 = jnp.float32
BF16 = jnp.bfloat16
SWAP = ((0, 1), (1, 0))
AHEAD = ((0, 1), (1, 2))
CROSS = ((1, 0), (0, 2))


def reverse(perm):
    return tuple((b, a) for a, b in perm)


def dp_shift(dx=0, dy=0):
    pairs = []
    for d in range(32):
        z, x, y = d // 16, (d // 4) % 4, d % 4
        pairs.append((d, z * 16 + ((x + dx) % 4) * 4 + (y + dy) % 4))
    return pairs


def pair_perm(flip):
    pairs = []
    for d in range(32):
        zl, rest = d // 16, d % 16
        for c in range(2):
            pairs.append((d * 2 + c, (c * 16 + rest) * 2 + (zl ^ flip)))
    return pairs


def dot(a, b, ca, cb):
    return lax.dot_general(a, b, (((ca,), (cb,)), ((), ())), preferred_element_type=F32)


def swap_halves(block):
    half = HD // 2
    return jnp.concatenate([block[:, half:], block[:, :half]], axis=1)


def kv_kernel(own_ref, recv_ref, cos_ref, sin_ref, kv_ref):
    cos, sin = cos_ref[...], sin_ref[...]
    for h in range(kv_ref.shape[1] // (2 * HD)):
        at = h * 2 * HD
        k = own_ref[:, at : at + HD] + recv_ref[:, at : at + HD]
        v = own_ref[:, at + HD : at + 2 * HD] + recv_ref[:, at + HD : at + 2 * HD]
        kv_ref[:, at : at + HD] = (k * cos + swap_halves(k) * sin).astype(BF16)
        kv_ref[:, at + HD : at + 2 * HD] = v.astype(BF16)


def attention_kernel(meta, q_ref, g_ref, kv_ref, a_ref, b_ref, own_ref, sa_ref, sb_ref):
    place, prefix, total = meta[0], meta[1], meta[2]
    starts = (
        place * TOK,
        jnp.where((place == 1) | (place == 2), (place - 1) * TOK, far_away),
        jnp.where(place == 0, TOK, jnp.where(place == 2, 0, far_away)),
    )
    rows = lax.broadcasted_iota(jnp.int32, (TOK, TOK), 0)
    query_at = place * TOK + lax.broadcasted_iota(jnp.int32, (TOK, TOK), 1)
    bias = []
    for start in starts:
        key_at = start + rows
        allowed = (key_at < total) & ((key_at < prefix) | (key_at <= query_at))
        bias.append(jnp.where(allowed, 0.0, neg_fill))
    bias = jnp.concatenate(bias, axis=0)
    live = jnp.where(query_at[0:1] < total, 1.0, 0.0)
    bias = jnp.concatenate([bias] * GROUP, axis=1)
    live = jnp.concatenate([live] * GROUP, axis=1)
    scale = HD ** (-0.5)
    blocks = (kv_ref, a_ref, b_ref)
    for h in range(kv_ref.shape[1] // (2 * HD)):
        at = h * 2 * HD
        keys = jnp.concatenate([r[:, at : at + HD] for r in blocks], axis=0)
        values = jnp.concatenate([r[:, at + HD : at + 2 * HD] for r in blocks], axis=0)
        cols = [slice((h * GROUP + i) * HD, (h * GROUP + i + 1) * HD) for i in range(GROUP)]
        queries = jnp.concatenate([q_ref[:, c] for c in cols], axis=0)
        grads = jnp.concatenate([g_ref[:, c] for c in cols], axis=0)
        scores = dot(keys, queries, 1, 1) * scale + bias
        top = jnp.max(scores, axis=0, keepdims=True)
        exponent = jnp.exp(scores - top)
        inverse = live / jnp.sum(exponent, axis=0, keepdims=True)
        attention = exponent * inverse
        grad_attention = dot(values, grads, 1, 1)
        delta = jnp.sum(attention * grad_attention, axis=0, keepdims=True)
        grad_scores = (attention * (grad_attention - delta)).astype(BF16)
        grad_values = dot(attention.astype(BF16), grads, 1, 0)
        grad_keys = dot(grad_scores, queries, 1, 0) * scale
        for ref, lo in ((own_ref, 0), (sa_ref, TOK), (sb_ref, 2 * TOK)):
            ref[:, at : at + HD] = grad_keys[lo : lo + TOK].astype(ref.dtype)
            ref[:, at + HD : at + 2 * HD] = grad_values[lo : lo + TOK].astype(ref.dtype)


def kg_kernel(own_ref, a_ref, b_ref, cos_ref, sin_ref, kg_ref):
    cos, sin = cos_ref[...], sin_ref[...]
    for h in range(kg_ref.shape[1] // (2 * HD)):
        at = h * 2 * HD
        ks, vs = slice(at, at + HD), slice(at + HD, at + 2 * HD)
        k = own_ref[:, ks] + a_ref[:, ks].astype(F32) + b_ref[:, ks].astype(F32)
        v = own_ref[:, vs] + a_ref[:, vs].astype(F32) + b_ref[:, vs].astype(F32)
        kg_ref[:, ks] = (k * cos - swap_halves(k) * sin).astype(BF16)
        kg_ref[:, vs] = v.astype(BF16)


def weight_kernel(meta, *refs):
    x_refs, k_refs, outs, total = refs[:4], refs[4:12], refs[12:16], refs[16]
    y = meta[0]
    left = jnp.concatenate([r[...] for r in x_refs], axis=0)
    right = jnp.concatenate([r[...] for r in k_refs], axis=0)
    total[...] = dot(left, right, 0, 0)
    rows = total.shape[0] // 4
    for k, out in enumerate(outs):
        at = pl.multiple_of(lax.rem(y + k, 4) * rows, 16)
        out[...] = total[pl.ds(at, rows), :].astype(out.dtype)


def sum_kernel(meta, own_ref, a_ref, b_ref, c_ref, same_ref, flip_ref):
    zl = meta[1]
    rows = same_ref.shape[0]
    total = own_ref[...] + a_ref[...].astype(F32) + b_ref[...].astype(F32) + c_ref[...].astype(F32)
    lower, upper = total[:rows].astype(BF16), total[rows:].astype(BF16)
    same_ref[...] = jnp.where(zl == 0, lower, upper)
    flip_ref[...] = jnp.where(zl == 0, upper, lower)


def call(kernel, outs, *args, meta=False, scratch=(), specs=None):
    if specs is None:
        specs = [VMEM] * len(args)
        if meta:
            specs[0] = SMEM
    return pl.pallas_call(
        kernel,
        out_shape=outs,
        in_specs=specs,
        out_specs=jax.tree.map(lambda _: VMEM, outs),
        scratch_shapes=scratch,
        compiler_params=PARAMS,
    )(*args)


def shape(rows, cols, dtype):
    return jax.ShapeDtypeStruct((rows, cols), dtype)


def on_device(layer_input, query, out_grad, camera_counts, action_counts, kv_weight):
    seq, core, dp = lax.axis_index("seq"), lax.axis_index("fsdp"), lax.axis_index("dp")
    zl, x, y = dp // 16, (dp // 4) % 4, dp % 4
    tokens, queries, grads = layer_input[0], query[0], out_grad[0]
    half = kv_weight.shape[0]
    width = kv_weight.shape[1]
    cols = width // NC
    prefix = camera_counts[0, 0] * IMG_TOK + TEXT
    total = prefix + action_counts[0, 0]
    meta = jnp.stack([seq, prefix, total]).astype(jnp.int32)
    spot = jnp.stack([y, zl]).astype(jnp.int32)

    position = (seq * TOK + jnp.arange(TOK, dtype=jnp.int32)).astype(F32)
    frequency = rope_base ** (-(2.0 * jnp.arange(HD // 2, dtype=F32)) / HD)
    angles = position[:, None] * frequency[None, :]
    cos, sin = jnp.cos(angles), jnp.sin(angles)
    cos = jnp.concatenate([cos, cos], axis=1)
    sin = jnp.concatenate([-sin, sin], axis=1)

    mine = lax.dynamic_slice_in_dim(tokens, core * half, half, 1)
    other = lax.ppermute(lax.dynamic_slice_in_dim(tokens, (1 - core) * half, half, 1), "fsdp", SWAP)
    part_mine = dot(mine, kv_weight, 1, 0)
    part_other = dot(other, kv_weight, 1, 0)

    pieces = []
    span = half // 4
    for k in range(4):
        at = ((x + k) % 4) * span
        piece = jnp.concatenate(
            [lax.dynamic_slice_in_dim(mine, at, span, 1), lax.dynamic_slice_in_dim(other, at, span, 1)], axis=0
        )
        pieces.append(piece if k == 0 else lax.ppermute(piece, "dp", dp_shift(dx=k)))

    kv, ahead, cross = [], [], []
    for c in range(NC):
        at = slice(c * cols, (c + 1) * cols)
        back = lax.ppermute(part_other[:, at], "fsdp", SWAP)
        kv.append(call(kv_kernel, shape(TOK, cols, BF16), part_mine[:, at], back, cos, sin))
        ahead.append(lax.ppermute(kv[c], "seq", AHEAD))
        cross.append(lax.ppermute(kv[c], "seq", CROSS))

    sums = []
    key_grads = []
    for c in range(NC):
        qcols = queries.shape[1] // NC
        qs = slice(c * qcols, (c + 1) * qcols)
        own, to_a, to_b = call(
            attention_kernel,
            (shape(TOK, cols, F32), shape(TOK, cols, BF16), shape(TOK, cols, BF16)),
            meta, queries[:, qs], grads[:, qs], kv[c], ahead[c], cross[c],
            meta=True,
        )
        from_a = lax.ppermute(to_a, "seq", reverse(AHEAD))
        from_b = lax.ppermute(to_b, "seq", reverse(CROSS))
        kg = call(kg_kernel, shape(TOK, cols, BF16), own, from_a, from_b, cos, sin)
        gathered = [kg] + [lax.ppermute(kg, "dp", dp_shift(dx=k)) for k in (1, 2, 3)]
        swapped = [lax.ppermute(g, "fsdp", SWAP) for g in gathered]
        key_grads.append((kg, swapped[0]))
        both = [a for pair in zip(gathered, swapped) for a in pair]
        rows = span // 4
        parts = call(
            weight_kernel,
            (shape(rows, cols, F32),) + (shape(rows, cols, BF16),) * 3,
            spot, *pieces, *both,
            meta=True,
            scratch=[pltpu.VMEM((span, cols), F32)],
        )
        came = [lax.ppermute(parts[k], "dp", dp_shift(dy=k)) for k in (1, 2, 3)]
        same, flip = call(
            sum_kernel, (shape(rows // 2, cols, BF16),) * 2, spot, parts[0], *came, meta=True
        )
        same = lax.ppermute(same, ("dp", "fsdp"), pair_perm(0))
        flip = lax.ppermute(flip, ("dp", "fsdp"), pair_perm(1))
        sums.append(same.astype(F32) + flip.astype(F32))

    summed = jnp.concatenate(sums, axis=1)
    out_cols = width // 4
    out = lax.dynamic_slice_in_dim(summed, seq * out_cols, out_cols, 1)
    for k in (1, 2, 3):
        piece = lax.dynamic_slice_in_dim(summed, ((seq + k) % 4) * out_cols, out_cols, 1).astype(BF16)
        perm = [(i, (i + k) % 4) for i in range(3)]
        out = out + lax.ppermute(piece, "seq", perm).astype(F32)

    kg = jnp.concatenate([a for a, _ in key_grads], axis=1)
    kg_other = jnp.concatenate([b for _, b in key_grads], axis=1)
    in_mine = dot(kg, kv_weight, 1, 1).astype(BF16)
    in_back = lax.ppermute(dot(kg_other, kv_weight, 1, 1).astype(BF16), "fsdp", SWAP)
    input_grad = jnp.where(
        core == 0,
        jnp.concatenate([in_mine, in_back], axis=1),
        jnp.concatenate([in_back, in_mine], axis=1),
    )
    return input_grad[None], out / lax.axis_size(("dp", "fsdp"))


def solution(mesh):
    placed = (
        P(("dp", "fsdp"), "seq", None),
        P(("dp", "fsdp"), "seq", None),
        P(("dp", "fsdp"), "seq", None),
        P(("dp", "fsdp"), None),
        P(("dp", "fsdp"), None),
        P("fsdp", None),
    )
    return jax.shard_map(
        on_device,
        mesh=mesh,
        in_specs=placed,
        out_specs=(P(("dp", "fsdp"), "seq", None), P(("dp", "fsdp"), "seq")),
        check_vma=False,
    )
```

```python
import jax
import jax.numpy as jnp
from jax import lax
from jax.experimental import pallas as pl
from jax.experimental.pallas import tpu as pltpu
from jax.sharding import PartitionSpec as P

HD = 128
GROUP = 5
IMG_TOK = 64
TEXT = 32
TOK = 128
TAIL = 32
TAIL_AT = 256
NG = 1
rope_base = 1000000.0
neg_fill = -1e30
VMEM = pl.BlockSpec(memory_space=pltpu.VMEM)
SMEM = pl.BlockSpec(memory_space=pltpu.SMEM)
F32 = jnp.float32
BF16 = jnp.bfloat16
SWAP = ((0, 1), (1, 0))
DOWN = ((0, 3), (1, 0), (2, 1), (3, 2))
UP = ((0, 1), (1, 2), (2, 3), (3, 0))
NEXT = ((0, 1), (1, 0), (2, 3), (3, 2))
ACROSS = ((0, 3), (1, 2), (2, 1), (3, 0))


def dp_shift(dx=0, dy=0, dz=0):
    pairs = []
    for d in range(32):
        z, x, y = d // 16, (d // 4) % 4, d % 4
        pairs.append((d, ((z + dz) % 2) * 16 + ((x + dx) % 4) * 4 + (y + dy) % 4))
    return pairs


def y_perm(dy):
    pairs = []
    for d in range(32):
        z, x, y = d // 16, (d // 4) % 4, d % 4
        for c in range(2):
            pairs.append((d * 2 + c, (c * 16 + x * 4 + (y + dy) % 4) * 2 + z))
    return pairs


def dot(a, b, ca, cb):
    return lax.dot_general(a, b, (((ca,), (cb,)), ((), ())), preferred_element_type=F32)


def swap_halves(block):
    half = HD // 2
    return jnp.concatenate([block[:, half:], block[:, :half]], axis=1)


def project_kernel(core, x_ref, w_ref, out_ref):
    half = w_ref.shape[0]
    out_ref[...] = dot(x_ref[:, pl.ds(pl.multiple_of(core[0] * half, HD), half)], w_ref[...], 1, 0)


def kv_kernel(own_ref, recv_ref, cos_ref, sin_ref, kv_ref, tail_ref):
    cos, sin = cos_ref[...], sin_ref[...]
    for h in range(kv_ref.shape[1] // (2 * HD)):
        at = h * 2 * HD
        ks, vs = slice(at, at + HD), slice(at + HD, at + 2 * HD)
        k = own_ref[:, ks] + recv_ref[:, ks]
        v = own_ref[:, vs] + recv_ref[:, vs]
        kv_ref[:, ks] = (k * cos + swap_halves(k) * sin).astype(BF16)
        kv_ref[:, vs] = v.astype(BF16)
    tail_ref[...] = kv_ref[:TAIL, :]


def attention_kernel(
    meta, q_ref, g_ref, tail_ref, kv_ref, next_ref, end_ref, own_out, next_out, end_out
):
    place, prefix, total = meta[0], meta[1], meta[2]
    n_own, n_all = GROUP * TOK, GROUP * (TOK + TAIL)
    n_keys = 2 * TOK + TAIL
    lane = lax.broadcasted_iota(jnp.int32, (1, n_all), 1)
    query_at = jnp.where(
        lane < n_own, place * TOK + lax.rem(lane, TOK), TAIL_AT + lax.rem(lane, TAIL)
    )
    live = (query_at < total) & (place < 2) & ((lane < n_own) | (place == 1))
    live = jnp.where(live, 1.0, 0.0)
    row = lax.broadcasted_iota(jnp.int32, (n_keys, 1), 0)
    key_at = jnp.where(
        row < TOK, place * TOK + row, jnp.where(row < 2 * TOK, (1 - place) * TOK + row - TOK, row)
    )
    key_at = jnp.where((row >= 2 * TOK) & (place != 1), total, key_at)
    allowed = (key_at < total) & ((key_at < prefix) | (key_at <= query_at))
    bias = jnp.where(allowed, 0.0, neg_fill)
    scale = HD ** (-0.5)
    width = tail_ref.shape[1] // 2
    for h in range(kv_ref.shape[1] // (2 * HD)):
        at = h * 2 * HD
        ks, vs = slice(at, at + HD), slice(at + HD, at + 2 * HD)

        def joined(cut):
            return jnp.concatenate([r[:, cut] for r in (kv_ref, next_ref, end_ref)], axis=0)

        keys, values = joined(ks), joined(vs)
        cols = [(h * GROUP + i) * HD for i in range(GROUP)]
        queries = jnp.concatenate(
            [q_ref[:, c : c + HD] for c in cols]
            + [tail_ref[:, c : c + HD] for c in cols],
            axis=0,
        )
        grads = jnp.concatenate(
            [g_ref[:, c : c + HD] for c in cols]
            + [tail_ref[:, width + c : width + c + HD] for c in cols],
            axis=0,
        )
        scores = dot(keys, queries, 1, 1) * scale + bias
        top = jnp.max(scores, axis=0, keepdims=True)
        exponent = jnp.exp(scores - top)
        inverse = live / jnp.sum(exponent, axis=0, keepdims=True)
        attention = exponent * inverse
        grad_attention = dot(values, grads, 1, 1)
        delta = jnp.sum(attention * grad_attention, axis=0, keepdims=True)
        grad_scores = (attention * (grad_attention - delta)).astype(BF16)
        grad_values = dot(attention.astype(BF16), grads, 1, 0)
        grad_keys = dot(grad_scores, queries, 1, 0) * scale
        for made, cut in ((grad_keys, ks), (grad_values, vs)):
            own_out[:, cut] = made[:TOK]
            next_out[:, cut] = made[TOK : 2 * TOK].astype(BF16)
            end_out[:, cut] = made[2 * TOK :].astype(BF16)


def kg_kernel(own_ref, next_ref, end_ref, cos_ref, sin_ref, *outs):
    cos, sin = cos_ref[...], sin_ref[...]
    cols = outs[0].shape[1]

    def total(cut):
        both = own_ref[:, cut] + next_ref[:, cut].astype(F32)
        return jnp.concatenate([both[:TAIL] + end_ref[:, cut].astype(F32), both[TAIL:]], axis=0)

    for c, out in enumerate(outs):
        for h in range(cols // (2 * HD)):
            at = h * 2 * HD
            k = total(slice(c * cols + at, c * cols + at + HD))
            out[:, at : at + HD] = (k * cos - swap_halves(k) * sin).astype(BF16)
            out[:, at + HD : at + 2 * HD] = total(
                slice(c * cols + at + HD, c * cols + at + 2 * HD)
            ).astype(BF16)


def weight_kernel(meta, *refs):
    mains, direct, swapped, outs, total = refs[:4], refs[4:8], refs[8:12], refs[12:16], refs[16]
    y = meta[0]
    left = jnp.concatenate([r[...] for r in mains], axis=0)
    right = jnp.concatenate([r[...] for pair in zip(direct, swapped) for r in pair], axis=0)
    total[...] = dot(left, right, 0, 0)
    rows = total.shape[0] // 4
    for k, out in enumerate(outs):
        out[...] = total[pl.ds(pl.multiple_of(lax.rem(y + k, 4) * rows, 16), rows), :].astype(BF16)


def sum_kernel(meta, a_ref, b_ref, c_ref, d_ref, keep_ref, give_ref):
    core = meta[1]
    rows = keep_ref.shape[0]
    total = a_ref[...].astype(F32) + b_ref[...].astype(F32)
    total = total + (c_ref[...].astype(F32) + d_ref[...].astype(F32))
    lower, upper = total[:rows], total[rows:]
    keep_ref[...] = jnp.where(core == 0, lower, upper)
    give_ref[...] = jnp.where(core == 0, upper, lower).astype(BF16)


def call(kernel, outs, *args, meta=False, scratch=(), cut=(), grid=(), vmem=40):
    specs = [VMEM] * len(args)
    if meta:
        specs[0] = SMEM
    for at, spec in cut:
        specs[at] = spec
    return pl.pallas_call(
        kernel,
        grid=grid,
        out_shape=outs,
        in_specs=specs,
        out_specs=jax.tree.map(lambda _: VMEM, outs),
        scratch_shapes=scratch,
        compiler_params=pltpu.CompilerParams(vmem_limit_bytes=vmem * 1024 * 1024),
    )(*args)


def shape(rows, cols, dtype):
    return jax.ShapeDtypeStruct((rows, cols), dtype)


def rope(position):
    frequency = rope_base ** (-(2.0 * jnp.arange(HD // 2, dtype=F32)) / HD)
    angles = position.astype(F32)[:, None] * frequency[None, :]
    cos, sin = jnp.cos(angles), jnp.sin(angles)
    return jnp.concatenate([cos, cos], axis=1), jnp.concatenate([-sin, sin], axis=1)


def on_device(layer_input, query, out_grad, camera_counts, action_counts, kv_weight):
    seq, core, dp = lax.axis_index("seq"), lax.axis_index("fsdp"), lax.axis_index("dp")
    x, y = (dp // 4) % 4, dp % 4
    tokens, queries, grads = layer_input[0], query[0], out_grad[0]
    half, width = kv_weight.shape
    prefix = camera_counts[0, 0] * IMG_TOK + TEXT
    total = prefix + action_counts[0, 0]
    meta = jnp.stack([seq, prefix, total]).astype(jnp.int32)
    spot = jnp.stack([y, core]).astype(jnp.int32)
    cos, sin = rope(seq * TOK + jnp.arange(TOK, dtype=jnp.int32))
    theirs = lax.ppermute(tokens, "fsdp", SWAP)
    which = core.astype(jnp.int32)[None]
    part_mine, part_other = [
        call(project_kernel, shape(TOK, width, F32), which, rows, kv_weight, meta=True)
        for rows in (tokens, theirs)
    ]
    tails = jnp.concatenate([queries[:TAIL], grads[:TAIL]], axis=1)
    back = lax.ppermute(part_other, "fsdp", SWAP)
    tails = lax.ppermute(tails, "seq", ACROSS)
    kv, kv_end = call(
        kv_kernel, (shape(TOK, width, BF16), shape(TAIL, width, BF16)), part_mine, back, cos, sin
    )
    kv_next = lax.ppermute(kv, "seq", NEXT)
    kv_end = lax.ppermute(kv_end, "seq", DOWN)

    span = half // 4
    kv, tokens, theirs = lax.optimization_barrier((kv, tokens, theirs))
    mains = []
    for k in range(4):
        at = core * half + ((x + k) % 4) * span
        mains.append(
            jnp.concatenate([lax.dynamic_slice_in_dim(r, at, span, 1) for r in (tokens, theirs)], axis=0)
        )
    tails, mains[2] = lax.optimization_barrier((tails, mains[2]))
    for k in (1, 2, 3):
        mains[k] = lax.ppermute(mains[k], "dp", dp_shift(dx=k))
    own, to_next, to_end = call(
        attention_kernel,
        (shape(TOK, width, F32), shape(TOK, width, BF16), shape(TAIL, width, BF16)),
        meta, queries, grads, tails, kv, kv_next, kv_end,
        meta=True,
    )
    from_next = lax.ppermute(to_next, "seq", NEXT)
    from_end = lax.ppermute(to_end, "seq", UP)
    from_next, mains = lax.optimization_barrier((from_next, mains))
    cols = width // NG
    kgs = call(kg_kernel, (shape(TOK, cols, BF16),) * NG, own, from_next, from_end, cos, sin)
    key_grads, finals = {}, {}
    for c in range(NG):
        kg = kgs[c]
        direct = [kg] + [lax.ppermute(kg, "dp", dp_shift(dx=k)) for k in (1, 2, 3)]
        swapped = [lax.ppermute(g, "fsdp", SWAP) for g in direct]
        rows = span // 4
        parts = call(
            weight_kernel, (shape(rows, cols, BF16),) * 4, spot, *mains, *direct, *swapped,
            meta=True,
            scratch=[pltpu.VMEM((span, cols), F32)],
        )
        parts = [lax.ppermute(p, ("dp", "fsdp"), y_perm(k)) for k, p in enumerate(parts)]
        key_grads[c] = (kg, swapped[0])
        if c == NG - 1:
            kg, kg_other = [jnp.concatenate([key_grads[i][j] for i in range(NG)], axis=1) for j in (0, 1)]
            in_mine = dot(kg, kv_weight, 1, 1).astype(BF16)
            in_back = lax.ppermute(dot(kg_other, kv_weight, 1, 1).astype(BF16), "fsdp", SWAP)
            parts[2], in_mine, in_back = lax.optimization_barrier((parts[2], in_mine, in_back))
        keep, give = call(
            sum_kernel, (shape(rows // 2, cols, F32), shape(rows // 2, cols, BF16)),
            spot, *parts, meta=True,
        )
        finals[c] = keep + lax.ppermute(give, "fsdp", SWAP).astype(F32)

    summed = jnp.concatenate([finals[c] for c in range(NG)], axis=1)
    head = width // 4
    parts = []
    for k in range(4):
        piece = lax.dynamic_slice_in_dim(summed, ((seq + k) % 4) * head, head, 1)
        parts.append(piece if k == 0 else piece.astype(BF16))
    for k in (2, 1, 3):
        parts[k] = lax.ppermute(parts[k], "seq", [(i, (i + k) % 4) for i in range(4)]).astype(F32)
    out = parts[0] + parts[1] + parts[2] + parts[3]

    input_grad = jnp.where(
        core == 0,
        jnp.concatenate([in_mine, in_back], axis=1),
        jnp.concatenate([in_back, in_mine], axis=1),
    )
    return input_grad[None], out / lax.axis_size(("dp", "fsdp"))


def solution(mesh):
    placed = (
        P(("dp", "fsdp"), "seq", None),
        P(("dp", "fsdp"), "seq", None),
        P(("dp", "fsdp"), "seq", None),
        P(("dp", "fsdp"), None),
        P(("dp", "fsdp"), None),
        P("fsdp", None),
    )
    return jax.shard_map(
        on_device,
        mesh=mesh,
        in_specs=placed,
        out_specs=(P(("dp", "fsdp"), "seq", None), P(("dp", "fsdp"), "seq")),
        check_vma=False,
    )
```

```python
import jax
import jax.numpy as jnp
from jax import lax
from jax.experimental import pallas as pl
from jax.experimental.pallas import tpu as pltpu
from jax.sharding import PartitionSpec as P

HD = 128
GROUP = 5
IMG_TOK = 64
TEXT = 32
TOK = 128
TAIL = 32
TAIL_AT = 256
NG = 1
rope_base = 1000000.0
neg_fill = -1e30
VMEM = pl.BlockSpec(memory_space=pltpu.VMEM)
SMEM = pl.BlockSpec(memory_space=pltpu.SMEM)
F32 = jnp.float32
BF16 = jnp.bfloat16
SWAP = ((0, 1), (1, 0))
TAIL_DOWN = ((2, 1),)
TAIL_BACK = ((1, 2),)
NEXT = ((0, 1), (1, 0), (2, 3), (3, 2))
ACROSS = ((0, 3), (1, 2), (2, 1), (3, 0))


def dp_shift(dx=0, dy=0, dz=0):
    pairs = []
    for d in range(32):
        z, x, y = d // 16, (d // 4) % 4, d % 4
        pairs.append((d, ((z + dz) % 2) * 16 + ((x + dx) % 4) * 4 + (y + dy) % 4))
    return pairs


def y_perm(dy):
    pairs = []
    for d in range(32):
        z, x, y = d // 16, (d // 4) % 4, d % 4
        for c in range(2):
            pairs.append((d * 2 + c, (c * 16 + x * 4 + (y + dy) % 4) * 2 + z))
    return pairs


def dot(a, b, ca, cb):
    return lax.dot_general(a, b, (((ca,), (cb,)), ((), ())), preferred_element_type=F32)


def swap_halves(block):
    half = HD // 2
    return jnp.concatenate([block[:, half:], block[:, :half]], axis=1)


def project_kernel(core, x_ref, w_ref, out_ref):
    half = w_ref.shape[0]
    out_ref[...] = dot(x_ref[:, pl.ds(pl.multiple_of(core[0] * half, HD), half)], w_ref[...], 1, 0)


def kv_kernel(own_ref, recv_ref, cos_ref, sin_ref, kv_ref, tail_ref):
    cos, sin = cos_ref[...], sin_ref[...]
    for h in range(kv_ref.shape[1] // (2 * HD)):
        at = h * 2 * HD
        ks, vs = slice(at, at + HD), slice(at + HD, at + 2 * HD)
        k = own_ref[:, ks] + recv_ref[:, ks]
        v = own_ref[:, vs] + recv_ref[:, vs]
        kv_ref[:, ks] = (k * cos + swap_halves(k) * sin).astype(BF16)
        kv_ref[:, vs] = v.astype(BF16)
    tail_ref[...] = kv_ref[:TAIL, :]


def attention_kernel(
    meta, q_ref, g_ref, tail_ref, kv_ref, next_ref, end_ref, own_out, next_out, end_out
):
    place, prefix, total = meta[0], meta[1], meta[2]
    n_own, n_all = GROUP * TOK, GROUP * (TOK + TAIL)
    n_keys = 2 * TOK + TAIL
    lane = lax.broadcasted_iota(jnp.int32, (1, n_all), 1)
    query_at = jnp.where(
        lane < n_own, place * TOK + lax.rem(lane, TOK), TAIL_AT + lax.rem(lane, TAIL)
    )
    live = (query_at < total) & (place < 2) & ((lane < n_own) | (place == 1))
    live = jnp.where(live, 1.0, 0.0)
    row = lax.broadcasted_iota(jnp.int32, (n_keys, 1), 0)
    key_at = jnp.where(
        row < TOK, place * TOK + row, jnp.where(row < 2 * TOK, (1 - place) * TOK + row - TOK, row)
    )
    key_at = jnp.where((row >= 2 * TOK) & (place != 1), total, key_at)
    allowed = (key_at < total) & ((key_at < prefix) | (key_at <= query_at))
    bias = jnp.where(allowed, 0.0, neg_fill)
    scale = HD ** (-0.5)
    width = tail_ref.shape[1] // 2
    for h in range(kv_ref.shape[1] // (2 * HD)):
        at = h * 2 * HD
        ks, vs = slice(at, at + HD), slice(at + HD, at + 2 * HD)

        def joined(cut):
            return jnp.concatenate([r[:, cut] for r in (kv_ref, next_ref, end_ref)], axis=0)

        keys, values = joined(ks), joined(vs)
        cols = [(h * GROUP + i) * HD for i in range(GROUP)]
        queries = jnp.concatenate(
            [q_ref[:, c : c + HD] for c in cols]
            + [tail_ref[:, c : c + HD] for c in cols],
            axis=0,
        )
        grads = jnp.concatenate(
            [g_ref[:, c : c + HD] for c in cols]
            + [tail_ref[:, width + c : width + c + HD] for c in cols],
            axis=0,
        )
        scores = dot(keys, queries, 1, 1) * scale + bias
        top = jnp.max(scores, axis=0, keepdims=True)
        exponent = jnp.exp(scores - top)
        inverse = live / jnp.sum(exponent, axis=0, keepdims=True)
        attention = exponent * inverse
        grad_attention = dot(values, grads, 1, 1)
        delta = jnp.sum(attention * grad_attention, axis=0, keepdims=True)
        grad_scores = (attention * (grad_attention - delta)).astype(BF16)
        grad_values = dot(attention.astype(BF16), grads, 1, 0)
        grad_keys = dot(grad_scores, queries, 1, 0) * scale
        for made, cut in ((grad_keys, ks), (grad_values, vs)):
            own_out[:, cut] = made[:TOK]
            next_out[:, cut] = made[TOK : 2 * TOK].astype(BF16)
            end_out[:, cut] = made[2 * TOK :].astype(BF16)


def kg_kernel(own_ref, next_ref, end_ref, cos_ref, sin_ref, *outs):
    cos, sin = cos_ref[...], sin_ref[...]
    cols = outs[0].shape[1]

    def total(cut):
        both = own_ref[:, cut] + next_ref[:, cut].astype(F32)
        return jnp.concatenate([both[:TAIL] + end_ref[:, cut].astype(F32), both[TAIL:]], axis=0)

    for c, out in enumerate(outs):
        for h in range(cols // (2 * HD)):
            at = h * 2 * HD
            k = total(slice(c * cols + at, c * cols + at + HD))
            out[:, at : at + HD] = (k * cos - swap_halves(k) * sin).astype(BF16)
            out[:, at + HD : at + 2 * HD] = total(
                slice(c * cols + at + HD, c * cols + at + 2 * HD)
            ).astype(BF16)


def weight_kernel(meta, *refs):
    mains, direct, swapped, outs, total = refs[:4], refs[4:8], refs[8:12], refs[12:16], refs[16]
    y = meta[0]
    left = jnp.concatenate([r[...] for r in mains], axis=0)
    right = jnp.concatenate([r[...] for pair in zip(direct, swapped) for r in pair], axis=0)
    total[...] = dot(left, right, 0, 0)
    rows = total.shape[0] // 4
    for k, out in enumerate(outs):
        out[...] = total[pl.ds(pl.multiple_of(lax.rem(y + k, 4) * rows, 16), rows), :].astype(BF16)


def sum_kernel(meta, a_ref, b_ref, c_ref, d_ref, keep_ref, give_ref):
    core = meta[1]
    rows = keep_ref.shape[0]
    total = a_ref[...].astype(F32) + b_ref[...].astype(F32)
    total = total + (c_ref[...].astype(F32) + d_ref[...].astype(F32))
    lower, upper = total[:rows], total[rows:]
    keep_ref[...] = jnp.where(core == 0, lower, upper)
    give_ref[...] = jnp.where(core == 0, upper, lower).astype(BF16)


def call(kernel, outs, *args, meta=False, scratch=(), cut=(), grid=(), vmem=40):
    specs = [VMEM] * len(args)
    if meta:
        specs[0] = SMEM
    for at, spec in cut:
        specs[at] = spec
    return pl.pallas_call(
        kernel,
        grid=grid,
        out_shape=outs,
        in_specs=specs,
        out_specs=jax.tree.map(lambda _: VMEM, outs),
        scratch_shapes=scratch,
        compiler_params=pltpu.CompilerParams(vmem_limit_bytes=vmem * 1024 * 1024),
    )(*args)


def shape(rows, cols, dtype):
    return jax.ShapeDtypeStruct((rows, cols), dtype)


def rope(position):
    frequency = rope_base ** (-(2.0 * jnp.arange(HD // 2, dtype=F32)) / HD)
    angles = position.astype(F32)[:, None] * frequency[None, :]
    cos, sin = jnp.cos(angles), jnp.sin(angles)
    return jnp.concatenate([cos, cos], axis=1), jnp.concatenate([-sin, sin], axis=1)


def on_device(layer_input, query, out_grad, camera_counts, action_counts, kv_weight):
    seq, core, dp = lax.axis_index("seq"), lax.axis_index("fsdp"), lax.axis_index("dp")
    x, y = (dp // 4) % 4, dp % 4
    tokens, queries, grads = layer_input[0], query[0], out_grad[0]
    half, width = kv_weight.shape
    prefix = camera_counts[0, 0] * IMG_TOK + TEXT
    total = prefix + action_counts[0, 0]
    meta = jnp.stack([seq, prefix, total]).astype(jnp.int32)
    spot = jnp.stack([y, core]).astype(jnp.int32)
    cos, sin = rope(seq * TOK + jnp.arange(TOK, dtype=jnp.int32))
    theirs = lax.ppermute(tokens, "fsdp", SWAP)
    which = core.astype(jnp.int32)[None]
    part_mine, part_other = [
        call(project_kernel, shape(TOK, width, F32), which, rows, kv_weight, meta=True)
        for rows in (tokens, theirs)
    ]
    tails = jnp.concatenate([queries[:TAIL], grads[:TAIL]], axis=1)
    back = lax.ppermute(part_other, "fsdp", SWAP)
    tails = lax.ppermute(tails, "seq", ACROSS)
    kv, kv_end = call(
        kv_kernel, (shape(TOK, width, BF16), shape(TAIL, width, BF16)), part_mine, back, cos, sin
    )
    kv_next = lax.ppermute(kv, "seq", NEXT)
    kv_end = lax.ppermute(kv_end, "seq", TAIL_DOWN)

    span = half // 4
    kv, tokens, theirs = lax.optimization_barrier((kv, tokens, theirs))
    mains = []
    for k in range(4):
        at = core * half + ((x + k) % 4) * span
        mains.append(
            jnp.concatenate([lax.dynamic_slice_in_dim(r, at, span, 1) for r in (tokens, theirs)], axis=0)
        )
    tails, mains[2] = lax.optimization_barrier((tails, mains[2]))
    for k in (1, 2, 3):
        mains[k] = lax.ppermute(mains[k], "dp", dp_shift(dx=k))
    own, to_next, to_end = call(
        attention_kernel,
        (shape(TOK, width, F32), shape(TOK, width, BF16), shape(TAIL, width, BF16)),
        meta, queries, grads, tails, kv, kv_next, kv_end,
        meta=True,
    )
    from_next = lax.ppermute(to_next, "seq", NEXT)
    from_end = lax.ppermute(to_end, "seq", TAIL_BACK)
    from_next, mains = lax.optimization_barrier((from_next, mains))
    cols = width // NG
    kgs = call(kg_kernel, (shape(TOK, cols, BF16),) * NG, own, from_next, from_end, cos, sin)
    key_grads, finals = {}, {}
    for c in range(NG):
        kg = kgs[c]
        direct = [kg] + [lax.ppermute(kg, "dp", dp_shift(dx=k)) for k in (1, 2, 3)]
        swapped = [lax.ppermute(g, "fsdp", SWAP) for g in direct]
        rows = span // 4
        parts = call(
            weight_kernel, (shape(rows, cols, BF16),) * 4, spot, *mains, *direct, *swapped,
            meta=True,
            scratch=[pltpu.VMEM((span, cols), F32)],
        )
        parts = [lax.ppermute(p, ("dp", "fsdp"), y_perm(k)) for k, p in enumerate(parts)]
        key_grads[c] = (kg, swapped[0])
        if c == NG - 1:
            kg, kg_other = [jnp.concatenate([key_grads[i][j] for i in range(NG)], axis=1) for j in (0, 1)]
            in_mine = dot(kg, kv_weight, 1, 1).astype(BF16)
            in_back = lax.ppermute(dot(kg_other, kv_weight, 1, 1).astype(BF16), "fsdp", SWAP)
            parts[2], in_mine, in_back = lax.optimization_barrier((parts[2], in_mine, in_back))
        keep, give = call(
            sum_kernel, (shape(rows // 2, cols, F32), shape(rows // 2, cols, BF16)),
            spot, *parts, meta=True,
        )
        finals[c] = keep + lax.ppermute(give, "fsdp", SWAP).astype(F32)

    summed = jnp.concatenate([finals[c] for c in range(NG)], axis=1)
    head = width // 4
    parts = []
    for k in range(4):
        piece = lax.dynamic_slice_in_dim(summed, ((seq + k) % 4) * head, head, 1)
        parts.append(piece if k == 0 else piece.astype(BF16))
    for k in (2, 1, 3):
        parts[k] = lax.ppermute(parts[k], "seq", [(i, (i + k) % 4) for i in range(4)]).astype(F32)
    out = parts[0] + parts[1] + parts[2] + parts[3]

    input_grad = jnp.where(
        core == 0,
        jnp.concatenate([in_mine, in_back], axis=1),
        jnp.concatenate([in_back, in_mine], axis=1),
    )
    return input_grad[None], out / lax.axis_size(("dp", "fsdp"))


def solution(mesh):
    placed = (
        P(("dp", "fsdp"), "seq", None),
        P(("dp", "fsdp"), "seq", None),
        P(("dp", "fsdp"), "seq", None),
        P(("dp", "fsdp"), None),
        P(("dp", "fsdp"), None),
        P("fsdp", None),
    )
    return jax.shard_map(
        on_device,
        mesh=mesh,
        in_specs=placed,
        out_specs=(P(("dp", "fsdp"), "seq", None), P(("dp", "fsdp"), "seq")),
        check_vma=False,
    )
```

```python
import jax
import jax.numpy as jnp
from jax import lax
from jax.experimental import pallas as pl
from jax.experimental.pallas import tpu as pltpu
from jax.sharding import PartitionSpec as P

HD = 128
GROUP = 5
IMG_TOK = 64
TEXT = 32
TOK = 128
TAIL = 32
TAIL_AT = 256
NG = 1
rope_base = 1000000.0
neg_fill = -1e30
VMEM = pl.BlockSpec(memory_space=pltpu.VMEM)
SMEM = pl.BlockSpec(memory_space=pltpu.SMEM)
F32 = jnp.float32
BF16 = jnp.bfloat16
SWAP = ((0, 1), (1, 0))
TAIL_DOWN = ((2, 1),)
TAIL_UP = ((2, 1), (3, 3))
TAIL_BACK = ((1, 2),)
NEXT = ((0, 1), (1, 0), (2, 3), (3, 2))
ACROSS = ((0, 3), (1, 2), (2, 1), (3, 0))


def dp_shift(dx=0, dy=0, dz=0):
    pairs = []
    for d in range(32):
        z, x, y = d // 16, (d // 4) % 4, d % 4
        pairs.append((d, ((z + dz) % 2) * 16 + ((x + dx) % 4) * 4 + (y + dy) % 4))
    return pairs


def y_perm(dy):
    pairs = []
    for d in range(32):
        z, x, y = d // 16, (d // 4) % 4, d % 4
        for c in range(2):
            pairs.append((d * 2 + c, (c * 16 + x * 4 + (y + dy) % 4) * 2 + z))
    return pairs


def dot(a, b, ca, cb):
    return lax.dot_general(a, b, (((ca,), (cb,)), ((), ())), preferred_element_type=F32)


def swap_halves(block):
    half = HD // 2
    return jnp.concatenate([block[:, half:], block[:, :half]], axis=1)


def project_kernel(core, x_ref, w_ref, out_ref):
    half = w_ref.shape[0]
    out_ref[...] = dot(x_ref[:, pl.ds(pl.multiple_of(core[0] * half, HD), half)], w_ref[...], 1, 0)


def kv_kernel(own_ref, recv_ref, cos_ref, sin_ref, kv_ref, tail_ref):
    cos, sin = cos_ref[...], sin_ref[...]
    for h in range(kv_ref.shape[1] // (2 * HD)):
        at = h * 2 * HD
        ks, vs = slice(at, at + HD), slice(at + HD, at + 2 * HD)
        k = own_ref[:, ks] + recv_ref[:, ks]
        v = own_ref[:, vs] + recv_ref[:, vs]
        kv_ref[:, ks] = (k * cos + swap_halves(k) * sin).astype(BF16)
        kv_ref[:, vs] = v.astype(BF16)
    tail_ref[...] = kv_ref[:TAIL, :]


def attention_kernel(
    meta, q_ref, g_ref, tail_ref, kv_ref, next_ref, end_ref, own_out, next_out, end_out
):
    place, prefix, total = meta[0], meta[1], meta[2]
    n_own, n_all = GROUP * TOK, GROUP * (TOK + TAIL)
    n_keys = 2 * TOK + TAIL
    lane = lax.broadcasted_iota(jnp.int32, (1, n_all), 1)
    query_at = jnp.where(
        lane < n_own, place * TOK + lax.rem(lane, TOK), TAIL_AT + lax.rem(lane, TAIL)
    )
    live = (query_at < total) & (place < 2) & ((lane < n_own) | (place == 1))
    live = jnp.where(live, 1.0, 0.0)
    row = lax.broadcasted_iota(jnp.int32, (n_keys, 1), 0)
    key_at = jnp.where(
        row < TOK, place * TOK + row, jnp.where(row < 2 * TOK, (1 - place) * TOK + row - TOK, row)
    )
    key_at = jnp.where((row >= 2 * TOK) & (place != 1), total, key_at)
    allowed = (key_at < total) & ((key_at < prefix) | (key_at <= query_at))
    bias = jnp.where(allowed, 0.0, neg_fill)
    scale = HD ** (-0.5)
    width = tail_ref.shape[1] // 2
    for h in range(kv_ref.shape[1] // (2 * HD)):
        at = h * 2 * HD
        ks, vs = slice(at, at + HD), slice(at + HD, at + 2 * HD)

        def joined(cut):
            return jnp.concatenate([r[:, cut] for r in (kv_ref, next_ref, end_ref)], axis=0)

        keys, values = joined(ks), joined(vs)
        cols = [(h * GROUP + i) * HD for i in range(GROUP)]
        queries = jnp.concatenate(
            [q_ref[:, c : c + HD] for c in cols]
            + [tail_ref[:, c : c + HD] for c in cols],
            axis=0,
        )
        grads = jnp.concatenate(
            [g_ref[:, c : c + HD] for c in cols]
            + [tail_ref[:, width + c : width + c + HD] for c in cols],
            axis=0,
        )
        scores = dot(keys, queries, 1, 1) * scale + bias
        top = jnp.max(scores, axis=0, keepdims=True)
        exponent = jnp.exp(scores - top)
        inverse = live / jnp.sum(exponent, axis=0, keepdims=True)
        attention = exponent * inverse
        grad_attention = dot(values, grads, 1, 1)
        delta = jnp.sum(attention * grad_attention, axis=0, keepdims=True)
        grad_scores = (attention * (grad_attention - delta)).astype(BF16)
        grad_values = dot(attention.astype(BF16), grads, 1, 0)
        grad_keys = dot(grad_scores, queries, 1, 0) * scale
        for made, cut in ((grad_keys, ks), (grad_values, vs)):
            own_out[:, cut] = made[:TOK]
            next_out[:, cut] = made[TOK : 2 * TOK].astype(BF16)
            end_out[:, cut] = made[2 * TOK :].astype(BF16)


def kg_kernel(own_ref, next_ref, end_ref, cos_ref, sin_ref, *outs):
    cos, sin = cos_ref[...], sin_ref[...]
    cols = outs[0].shape[1]

    def total(cut):
        both = own_ref[:, cut] + next_ref[:, cut].astype(F32)
        return jnp.concatenate([both[:TAIL] + end_ref[:, cut].astype(F32), both[TAIL:]], axis=0)

    for c, out in enumerate(outs):
        for h in range(cols // (2 * HD)):
            at = h * 2 * HD
            k = total(slice(c * cols + at, c * cols + at + HD))
            out[:, at : at + HD] = (k * cos - swap_halves(k) * sin).astype(BF16)
            out[:, at + HD : at + 2 * HD] = total(
                slice(c * cols + at + HD, c * cols + at + 2 * HD)
            ).astype(BF16)


def weight_kernel(meta, *refs):
    mains, direct, swapped, outs, total = refs[:4], refs[4:8], refs[8:12], refs[12:16], refs[16]
    y = meta[0]
    left = jnp.concatenate([r[...] for r in mains], axis=0)
    right = jnp.concatenate([r[...] for pair in zip(direct, swapped) for r in pair], axis=0)
    total[...] = dot(left, right, 0, 0)
    rows = total.shape[0] // 4
    for k, out in enumerate(outs):
        out[...] = total[pl.ds(pl.multiple_of(lax.rem(y + k, 4) * rows, 16), rows), :].astype(BF16)


def sum_kernel(meta, a_ref, b_ref, c_ref, d_ref, keep_ref, give_ref):
    core = meta[1]
    rows = keep_ref.shape[0]
    total = a_ref[...].astype(F32) + b_ref[...].astype(F32)
    total = total + (c_ref[...].astype(F32) + d_ref[...].astype(F32))
    lower, upper = total[:rows], total[rows:]
    keep_ref[...] = jnp.where(core == 0, lower, upper)
    give_ref[...] = jnp.where(core == 0, upper, lower).astype(BF16)


def call(kernel, outs, *args, meta=False, scratch=(), cut=(), grid=(), vmem=40):
    specs = [VMEM] * len(args)
    if meta:
        specs[0] = SMEM
    for at, spec in cut:
        specs[at] = spec
    return pl.pallas_call(
        kernel,
        grid=grid,
        out_shape=outs,
        in_specs=specs,
        out_specs=jax.tree.map(lambda _: VMEM, outs),
        scratch_shapes=scratch,
        compiler_params=pltpu.CompilerParams(vmem_limit_bytes=vmem * 1024 * 1024),
    )(*args)


def shape(rows, cols, dtype):
    return jax.ShapeDtypeStruct((rows, cols), dtype)


def rope(position):
    frequency = rope_base ** (-(2.0 * jnp.arange(HD // 2, dtype=F32)) / HD)
    angles = position.astype(F32)[:, None] * frequency[None, :]
    cos, sin = jnp.cos(angles), jnp.sin(angles)
    return jnp.concatenate([cos, cos], axis=1), jnp.concatenate([-sin, sin], axis=1)


def on_device(layer_input, query, out_grad, camera_counts, action_counts, kv_weight):
    seq, core, dp = lax.axis_index("seq"), lax.axis_index("fsdp"), lax.axis_index("dp")
    x, y = (dp // 4) % 4, dp % 4
    tokens, queries, grads = layer_input[0], query[0], out_grad[0]
    half, width = kv_weight.shape
    prefix = camera_counts[0, 0] * IMG_TOK + TEXT
    total = prefix + action_counts[0, 0]
    meta = jnp.stack([seq, prefix, total]).astype(jnp.int32)
    spot = jnp.stack([y, core]).astype(jnp.int32)
    cos, sin = rope(seq * TOK + jnp.arange(TOK, dtype=jnp.int32))
    theirs = lax.ppermute(tokens, "fsdp", SWAP)
    which = core.astype(jnp.int32)[None]
    part_mine, part_other = [
        call(project_kernel, shape(TOK, width, F32), which, rows, kv_weight, meta=True)
        for rows in (tokens, theirs)
    ]
    tails = jnp.concatenate([queries[:TAIL], grads[:TAIL]], axis=1)
    back = lax.ppermute(part_other, "fsdp", SWAP)
    tails = lax.ppermute(tails, "seq", TAIL_UP)
    kv, kv_end = call(
        kv_kernel, (shape(TOK, width, BF16), shape(TAIL, width, BF16)), part_mine, back, cos, sin
    )
    kv_next = lax.ppermute(kv, "seq", NEXT)
    kv_end = lax.ppermute(kv_end, "seq", TAIL_DOWN)

    span = half // 4
    kv, tokens, theirs = lax.optimization_barrier((kv, tokens, theirs))
    mains = []
    for k in range(4):
        at = core * half + ((x + k) % 4) * span
        mains.append(
            jnp.concatenate([lax.dynamic_slice_in_dim(r, at, span, 1) for r in (tokens, theirs)], axis=0)
        )
    tails, mains[2] = lax.optimization_barrier((tails, mains[2]))
    for k in (1, 2, 3):
        mains[k] = lax.ppermute(mains[k], "dp", dp_shift(dx=k))
    own, to_next, to_end = call(
        attention_kernel,
        (shape(TOK, width, F32), shape(TOK, width, BF16), shape(TAIL, width, BF16)),
        meta, queries, grads, tails, kv, kv_next, kv_end,
        meta=True,
    )
    from_next = lax.ppermute(to_next, "seq", NEXT)
    from_end = lax.ppermute(to_end, "seq", TAIL_BACK)
    from_next, mains = lax.optimization_barrier((from_next, mains))
    cols = width // NG
    kgs = call(kg_kernel, (shape(TOK, cols, BF16),) * NG, own, from_next, from_end, cos, sin)
    key_grads, finals = {}, {}
    for c in range(NG):
        kg = kgs[c]
        direct = [kg] + [lax.ppermute(kg, "dp", dp_shift(dx=k)) for k in (1, 2, 3)]
        swapped = [lax.ppermute(g, "fsdp", SWAP) for g in direct]
        rows = span // 4
        parts = call(
            weight_kernel, (shape(rows, cols, BF16),) * 4, spot, *mains, *direct, *swapped,
            meta=True,
            scratch=[pltpu.VMEM((span, cols), F32)],
        )
        parts = [lax.ppermute(p, ("dp", "fsdp"), y_perm(k)) for k, p in enumerate(parts)]
        key_grads[c] = (kg, swapped[0])
        if c == NG - 1:
            kg, kg_other = [jnp.concatenate([key_grads[i][j] for i in range(NG)], axis=1) for j in (0, 1)]
            in_mine = dot(kg, kv_weight, 1, 1).astype(BF16)
            in_back = lax.ppermute(dot(kg_other, kv_weight, 1, 1).astype(BF16), "fsdp", SWAP)
            parts[2], in_mine, in_back = lax.optimization_barrier((parts[2], in_mine, in_back))
        keep, give = call(
            sum_kernel, (shape(rows // 2, cols, F32), shape(rows // 2, cols, BF16)),
            spot, *parts, meta=True,
        )
        finals[c] = keep + lax.ppermute(give, "fsdp", SWAP).astype(F32)

    summed = jnp.concatenate([finals[c] for c in range(NG)], axis=1)
    head = width // 4
    parts = []
    for k in range(4):
        piece = lax.dynamic_slice_in_dim(summed, (seq ^ k) * head, head, 1)
        parts.append(piece if k == 0 else piece.astype(BF16))
    for k in (2, 1, 3):
        parts[k] = lax.ppermute(parts[k], "seq", [(i, i ^ k) for i in range(4)]).astype(F32)
    out = parts[0] + parts[1] + parts[2] + parts[3]

    input_grad = jnp.where(
        core == 0,
        jnp.concatenate([in_mine, in_back], axis=1),
        jnp.concatenate([in_back, in_mine], axis=1),
    )
    return input_grad[None], out / lax.axis_size(("dp", "fsdp"))


def solution(mesh):
    placed = (
        P(("dp", "fsdp"), "seq", None),
        P(("dp", "fsdp"), "seq", None),
        P(("dp", "fsdp"), "seq", None),
        P(("dp", "fsdp"), None),
        P(("dp", "fsdp"), None),
        P("fsdp", None),
    )
    return jax.shard_map(
        on_device,
        mesh=mesh,
        in_specs=placed,
        out_specs=(P(("dp", "fsdp"), "seq", None), P(("dp", "fsdp"), "seq")),
        check_vma=False,
    )
```

```python
import jax
import jax.numpy as jnp
from jax import lax
from jax.experimental import pallas as pl
from jax.experimental.pallas import tpu as pltpu
from jax.sharding import PartitionSpec as P

HD = 128
GROUP = 5
IMG_TOK = 64
TEXT = 32
TOK = 128
TAIL = 32
TAIL_AT = 256
NG = 1
rope_base = 1000000.0
neg_fill = -1e30
VMEM = pl.BlockSpec(memory_space=pltpu.VMEM)
SMEM = pl.BlockSpec(memory_space=pltpu.SMEM)
F32 = jnp.float32
BF16 = jnp.bfloat16
SWAP = ((0, 1), (1, 0))
TAIL_DOWN = ((2, 1),)
TAIL_UP = ((2, 1), (3, 3))
TAIL_BACK = ((1, 2),)
NEXT = ((0, 1), (1, 0), (2, 3), (3, 2))
ACROSS = ((0, 3), (1, 2), (2, 1), (3, 0))


def dp_shift(dx=0, dy=0, dz=0):
    pairs = []
    for d in range(32):
        z, x, y = d // 16, (d // 4) % 4, d % 4
        pairs.append((d, ((z + dz) % 2) * 16 + ((x + dx) % 4) * 4 + (y + dy) % 4))
    return pairs


def y_perm(dy):
    pairs = []
    for d in range(32):
        z, x, y = d // 16, (d // 4) % 4, d % 4
        for c in range(2):
            pairs.append((d * 2 + c, (c * 16 + x * 4 + (y + dy) % 4) * 2 + z))
    return pairs


def dot(a, b, ca, cb):
    return lax.dot_general(a, b, (((ca,), (cb,)), ((), ())), preferred_element_type=F32)


def swap_halves(block):
    half = HD // 2
    return jnp.concatenate([block[:, half:], block[:, :half]], axis=1)


def project_kernel(core, x_ref, w_ref, out_ref):
    half = w_ref.shape[0]
    out_ref[...] = dot(x_ref[:, pl.ds(pl.multiple_of(core[0] * half, HD), half)], w_ref[...], 1, 0)


def kv_kernel(own_ref, recv_ref, cos_ref, sin_ref, kv_ref, tail_ref):
    cos, sin = cos_ref[...], sin_ref[...]
    for h in range(kv_ref.shape[1] // (2 * HD)):
        at = h * 2 * HD
        ks, vs = slice(at, at + HD), slice(at + HD, at + 2 * HD)
        k = own_ref[:, ks] + recv_ref[:, ks]
        v = own_ref[:, vs] + recv_ref[:, vs]
        kv_ref[:, ks] = (k * cos + swap_halves(k) * sin).astype(BF16)
        kv_ref[:, vs] = v.astype(BF16)
    tail_ref[...] = kv_ref[:TAIL, :]


def attention_kernel(
    meta, q_ref, g_ref, tail_ref, kv_ref, next_ref, end_ref, own_out, next_out, end_out
):
    place, prefix, total = meta[0], meta[1], meta[2]
    n_own, n_all = GROUP * TOK, GROUP * (TOK + TAIL)
    n_keys = 2 * TOK + TAIL
    lane = lax.broadcasted_iota(jnp.int32, (1, n_all), 1)
    query_at = jnp.where(
        lane < n_own, place * TOK + lax.rem(lane, TOK), TAIL_AT + lax.rem(lane, TAIL)
    )
    live = (query_at < total) & (place < 2) & ((lane < n_own) | (place == 1))
    live = jnp.where(live, 1.0, 0.0)
    row = lax.broadcasted_iota(jnp.int32, (n_keys, 1), 0)
    key_at = jnp.where(
        row < TOK, place * TOK + row, jnp.where(row < 2 * TOK, (1 - place) * TOK + row - TOK, row)
    )
    key_at = jnp.where((row >= 2 * TOK) & (place != 1), total, key_at)
    allowed = (key_at < total) & ((key_at < prefix) | (key_at <= query_at))
    bias = jnp.where(allowed, 0.0, neg_fill)
    scale = HD ** (-0.5)
    width = tail_ref.shape[1] // 2
    for h in range(kv_ref.shape[1] // (2 * HD)):
        at = h * 2 * HD
        ks, vs = slice(at, at + HD), slice(at + HD, at + 2 * HD)

        def joined(cut):
            return jnp.concatenate([r[:, cut] for r in (kv_ref, next_ref, end_ref)], axis=0)

        keys, values = joined(ks), joined(vs)
        cols = [(h * GROUP + i) * HD for i in range(GROUP)]
        queries = jnp.concatenate(
            [q_ref[:, c : c + HD] for c in cols]
            + [tail_ref[:, c : c + HD] for c in cols],
            axis=0,
        )
        grads = jnp.concatenate(
            [g_ref[:, c : c + HD] for c in cols]
            + [tail_ref[:, width + c : width + c + HD] for c in cols],
            axis=0,
        )
        scores = dot(keys, queries, 1, 1) * scale + bias
        top = jnp.max(scores, axis=0, keepdims=True)
        exponent = jnp.exp(scores - top)
        inverse = live / jnp.sum(exponent, axis=0, keepdims=True)
        attention = exponent * inverse
        grad_attention = dot(values, grads, 1, 1)
        delta = jnp.sum(attention * grad_attention, axis=0, keepdims=True)
        grad_scores = (attention * (grad_attention - delta)).astype(BF16)
        grad_values = dot(attention.astype(BF16), grads, 1, 0)
        grad_keys = dot(grad_scores, queries, 1, 0) * scale
        for made, cut in ((grad_keys, ks), (grad_values, vs)):
            own_out[:, cut] = made[:TOK]
            next_out[:, cut] = made[TOK : 2 * TOK].astype(BF16)
            end_out[:, cut] = made[2 * TOK :].astype(BF16)


def kg_kernel(own_ref, next_ref, end_ref, cos_ref, sin_ref, *outs):
    cos, sin = cos_ref[...], sin_ref[...]
    cols = outs[0].shape[1]

    def total(cut):
        both = own_ref[:, cut] + next_ref[:, cut].astype(F32)
        return jnp.concatenate([both[:TAIL] + end_ref[:, cut].astype(F32), both[TAIL:]], axis=0)

    for c, out in enumerate(outs):
        for h in range(cols // (2 * HD)):
            at = h * 2 * HD
            k = total(slice(c * cols + at, c * cols + at + HD))
            out[:, at : at + HD] = (k * cos - swap_halves(k) * sin).astype(BF16)
            out[:, at + HD : at + 2 * HD] = total(
                slice(c * cols + at + HD, c * cols + at + 2 * HD)
            ).astype(BF16)


def weight_kernel(meta, *refs):
    mains, direct, swapped, outs, total = refs[:4], refs[4:8], refs[8:12], refs[12:16], refs[16]
    y = meta[0]
    left = jnp.concatenate([r[...] for r in mains], axis=0)
    right = jnp.concatenate([r[...] for pair in zip(direct, swapped) for r in pair], axis=0)
    total[...] = dot(left, right, 0, 0)
    rows = total.shape[0] // 4
    for k, out in enumerate(outs):
        out[...] = total[pl.ds(pl.multiple_of(lax.rem(y + k, 4) * rows, 16), rows), :].astype(BF16)


def sum_kernel(meta, a_ref, b_ref, c_ref, d_ref, keep_ref, give_ref):
    core = meta[1]
    rows = keep_ref.shape[0]
    total = a_ref[...].astype(F32) + b_ref[...].astype(F32)
    total = total + (c_ref[...].astype(F32) + d_ref[...].astype(F32))
    lower, upper = total[:rows], total[rows:]
    keep_ref[...] = jnp.where(core == 0, lower, upper)
    give_ref[...] = jnp.where(core == 0, upper, lower).astype(BF16)


def call(kernel, outs, *args, meta=False, scratch=(), cut=(), grid=(), vmem=40):
    specs = [VMEM] * len(args)
    if meta:
        specs[0] = SMEM
    for at, spec in cut:
        specs[at] = spec
    return pl.pallas_call(
        kernel,
        grid=grid,
        out_shape=outs,
        in_specs=specs,
        out_specs=jax.tree.map(lambda _: VMEM, outs),
        scratch_shapes=scratch,
        compiler_params=pltpu.CompilerParams(vmem_limit_bytes=vmem * 1024 * 1024),
    )(*args)


def shape(rows, cols, dtype):
    return jax.ShapeDtypeStruct((rows, cols), dtype)


def rope(position):
    frequency = rope_base ** (-(2.0 * jnp.arange(HD // 2, dtype=F32)) / HD)
    angles = position.astype(F32)[:, None] * frequency[None, :]
    cos, sin = jnp.cos(angles), jnp.sin(angles)
    return jnp.concatenate([cos, cos], axis=1), jnp.concatenate([-sin, sin], axis=1)


def on_device(layer_input, query, out_grad, camera_counts, action_counts, kv_weight):
    seq, core, dp = lax.axis_index("seq"), lax.axis_index("fsdp"), lax.axis_index("dp")
    x, y = (dp // 4) % 4, dp % 4
    tokens, queries, grads = layer_input[0], query[0], out_grad[0]
    half, width = kv_weight.shape
    prefix = camera_counts[0, 0] * IMG_TOK + TEXT
    total = prefix + action_counts[0, 0]
    meta = jnp.stack([seq, prefix, total]).astype(jnp.int32)
    spot = jnp.stack([y, core]).astype(jnp.int32)
    cos, sin = rope(seq * TOK + jnp.arange(TOK, dtype=jnp.int32))
    theirs = lax.ppermute(tokens, "fsdp", SWAP)
    which = core.astype(jnp.int32)[None]
    part_mine, part_other = [
        call(project_kernel, shape(TOK, width, F32), which, rows, kv_weight, meta=True)
        for rows in (tokens, theirs)
    ]
    tails = jnp.concatenate([queries[:TAIL], grads[:TAIL]], axis=1)
    back = lax.ppermute(part_other, "fsdp", SWAP)
    tails = lax.ppermute(tails, "seq", TAIL_UP)
    kv, kv_end = call(
        kv_kernel, (shape(TOK, width, BF16), shape(TAIL, width, BF16)), part_mine, back, cos, sin
    )
    kv_next = lax.ppermute(kv, "seq", NEXT)
    kv_end = lax.ppermute(kv_end, "seq", TAIL_DOWN)

    span = half // 4
    kv, tokens, theirs = lax.optimization_barrier((kv, tokens, theirs))
    mains = []
    for k in range(4):
        at = core * half + ((x + k) % 4) * span
        mains.append(
            jnp.concatenate([lax.dynamic_slice_in_dim(r, at, span, 1) for r in (tokens, theirs)], axis=0)
        )
    for k in (1, 2, 3):
        mains[k] = lax.ppermute(mains[k], "dp", dp_shift(dx=k))
    own, to_next, to_end = call(
        attention_kernel,
        (shape(TOK, width, F32), shape(TOK, width, BF16), shape(TAIL, width, BF16)),
        meta, queries, grads, tails, kv, kv_next, kv_end,
        meta=True,
    )
    from_next = lax.ppermute(to_next, "seq", NEXT)
    from_end = lax.ppermute(to_end, "seq", TAIL_BACK)
    from_next, mains = lax.optimization_barrier((from_next, mains))
    cols = width // NG
    kgs = call(kg_kernel, (shape(TOK, cols, BF16),) * NG, own, from_next, from_end, cos, sin)
    key_grads, finals = {}, {}
    for c in range(NG):
        kg = kgs[c]
        direct = [kg] + [lax.ppermute(kg, "dp", dp_shift(dx=k)) for k in (1, 2, 3)]
        swapped = [lax.ppermute(g, "fsdp", SWAP) for g in direct]
        rows = span // 4
        parts = call(
            weight_kernel, (shape(rows, cols, BF16),) * 4, spot, *mains, *direct, *swapped,
            meta=True,
            scratch=[pltpu.VMEM((span, cols), F32)],
        )
        parts = [lax.ppermute(p, ("dp", "fsdp"), y_perm(k)) for k, p in enumerate(parts)]
        key_grads[c] = (kg, swapped[0])
        if c == NG - 1:
            kg, kg_other = [jnp.concatenate([key_grads[i][j] for i in range(NG)], axis=1) for j in (0, 1)]
            in_mine = dot(kg, kv_weight, 1, 1).astype(BF16)
            in_back = lax.ppermute(dot(kg_other, kv_weight, 1, 1).astype(BF16), "fsdp", SWAP)
            parts[2], in_mine, in_back = lax.optimization_barrier((parts[2], in_mine, in_back))
        keep, give = call(
            sum_kernel, (shape(rows // 2, cols, F32), shape(rows // 2, cols, BF16)),
            spot, *parts, meta=True,
        )
        finals[c] = keep + lax.ppermute(give, "fsdp", SWAP).astype(F32)

    summed = jnp.concatenate([finals[c] for c in range(NG)], axis=1)
    head = width // 4
    parts = []
    for k in range(4):
        piece = lax.dynamic_slice_in_dim(summed, (seq ^ k) * head, head, 1)
        parts.append(piece if k == 0 else piece.astype(BF16))
    for k in (2, 1, 3):
        parts[k] = lax.ppermute(parts[k], "seq", [(i, i ^ k) for i in range(4)]).astype(F32)
    out = parts[0] + parts[1] + parts[2] + parts[3]

    input_grad = jnp.where(
        core == 0,
        jnp.concatenate([in_mine, in_back], axis=1),
        jnp.concatenate([in_back, in_mine], axis=1),
    )
    return input_grad[None], out / lax.axis_size(("dp", "fsdp"))


def solution(mesh):
    placed = (
        P(("dp", "fsdp"), "seq", None),
        P(("dp", "fsdp"), "seq", None),
        P(("dp", "fsdp"), "seq", None),
        P(("dp", "fsdp"), None),
        P(("dp", "fsdp"), None),
        P("fsdp", None),
    )
    return jax.shard_map(
        on_device,
        mesh=mesh,
        in_specs=placed,
        out_specs=(P(("dp", "fsdp"), "seq", None), P(("dp", "fsdp"), "seq")),
        check_vma=False,
    )
```
